32 devices in a mesh: section: 4 (over x, core), space: 8 (over z, y).
Axes of the slice: x: 2, y: 2, z: 4, core: 2. Of those that a mesh axis runs over, the one named last changes fastest.
Arguments:
- frames: bfloat16 [4, 4, 128, 96, 128], P('section', None, 'space'), may hold values from -6 to 6
- patch_weight: bfloat16 [2, 256, 128], replicated, may hold values from -0.25 to 0.25
- patch_bias: float32 [128], replicated, may hold values from -3 to 3
- enc_weight: bfloat16 [1152, 128], replicated, may hold values from -0.1875 to 0.1875
- cell_weight: bfloat16 [4, 2304, 512], P('section'), may hold values from -0.125 to 1.25
- cell_bias: float32 [4, 512], P('section'), may hold values from -3 to 4
- head_weight: bfloat16 [3, 1152, 128], replicated, may hold values from -0.1875 to 0.1875
- out_weight: bfloat16 [128, 512], replicated, may hold values from -0.5 to 0.5
- out_bias: float32 [512], replicated, may hold values from -2 to 2
Outputs:
- logits: bfloat16 [4, 4, 64, 48, 512], P('section', None, 'space')
The draws below stay inside these ranges and needn't reach their ends.
All inputs are finite; a program needn't handle non-finite values.
Results may differ from the reference program's by a relative error of at most 0.015.
Values may be sent and summed in bfloat16 or wider, within the bound.
A program may use at most 64 MiB of HBM per device.

```python
import math
import jax
import jax.numpy as jnp

C = 128
CIN = 128
BINS = 512
STEPS = 4
COLS = 48
MB = 4
LAYERS = 4
NROWS = 64


def coupling(key, first_layer):
    direction = jax.random.randint(key, (C,), 0, 2)
    row_ids = jnp.arange(18 * C, dtype=jnp.int32)[:, None]
    col_ids = jnp.arange(4 * C, dtype=jnp.int32)[None, :]
    channel = col_ids - 2 * C
    in_cand = (channel >= 0) & (channel < C)
    channel = jnp.clip(channel, 0, C - 1)
    offset = 2 * C + 12 * C * direction[channel]
    from_input = ((row_ids == offset + channel) & in_cand).astype(jnp.float32)
    from_hidden = ((row_ids == offset + C + channel) & in_cand).astype(jnp.float32)
    layer_scale = jnp.where(jnp.arange(LAYERS) == 0, first_layer, 1.0).astype(jnp.float32)
    return from_hidden[None] + layer_scale[:, None, None] * from_input[None]


def draw_cell_weight(key, part):
    key = jax.random.fold_in(key, 11)
    random_key, direction_key = jax.random.split(key)
    spread = 0.7 / math.sqrt(18 * C)
    random_part = jnp.clip(jax.random.normal(random_key, (LAYERS, 18 * C, 4 * C), jnp.float32), -4.0, 4.0) * spread
    coupled = coupling(direction_key, 0.4)
    return (random_part + coupled).astype(jnp.bfloat16)


def draw_cell_bias(key, part):
    key = jax.random.fold_in(key, 12)
    subkeys = jax.random.split(key, 4)
    open_low, open_high, keep_low, keep_high, spread = (2.0, 3.5, -2.0, 1.0, 0.5)
    input_gate = jax.random.uniform(subkeys[0], (LAYERS, C), jnp.float32, open_low, open_high)
    forget_gate = jax.random.uniform(subkeys[1], (LAYERS, C), jnp.float32, keep_low, keep_high)
    candidate = jnp.clip(jax.random.normal(subkeys[2], (LAYERS, C), jnp.float32) * spread, -1.5, 1.5)
    output_gate = jax.random.uniform(subkeys[3], (LAYERS, C), jnp.float32, open_low, open_high)
    return jnp.concatenate([input_gate, forget_gate, candidate, output_gate], -1)


def block_scale(stream_key, shape, cuts, low, top_value):
    level = 1.0
    for dim, blocks in cuts:
        steps = jax.random.uniform(jax.random.fold_in(jax.random.fold_in(stream_key, 6), dim), (blocks,), jnp.float32, low / len(cuts), top_value / len(cuts))
        level = level * jnp.repeat(jnp.exp(steps), shape[dim] // blocks).reshape((-1,) + (1,) * (len(shape) - 1 - dim))
    return level


def scatter_about(rng, dims, deviation, reach, cuts=(), held_as=jnp.bfloat16):
    loudness = block_scale(rng, dims, cuts, -0.22, 0.18) if cuts else 1.0
    values = jax.random.normal(rng, dims, jnp.float32) * deviation * loudness
    return jnp.minimum(jnp.maximum(values, -reach), reach).astype(held_as)


def setup_inputs(seed: int = 0) -> dict:
    key_list = jax.random.split(jax.random.key(seed), 10)
    return {
        "frames": scatter_about(key_list[0], (MB, STEPS, 2 * NROWS, 2 * COLS, CIN), 1.0, 6.0, ((0, 4), (2, 8))),
        "patch_weight": scatter_about(key_list[1], (2, 2 * CIN, C), (4 * CIN) ** -0.5, 0.25),
        "patch_bias": scatter_about(key_list[2], (C,), 0.5, 3.0, (), jnp.float32),
        "enc_weight": scatter_about(key_list[3], (9 * C, C), (9 * C) ** -0.5, 0.1875),
        "cell_weight": draw_cell_weight(jax.random.fold_in(key_list[9], 71), 0),
        "cell_bias": draw_cell_bias(jax.random.fold_in(key_list[9], 71), 0),
        "head_weight": scatter_about(key_list[6], (3, 9 * C, C), (9 * C) ** -0.5, 0.1875),
        "out_weight": scatter_about(key_list[7], (C, BINS), C ** -0.5, 0.5),
        "out_bias": scatter_about(key_list[8], (BINS,), 0.5, 2.0, (), jnp.float32),
    }


def dilated(padded, weight, spacing):
    row_count = padded.shape[-3] - 2 * spacing
    col_count = padded.shape[-2]
    widths = [(0, 0)] * (padded.ndim - 2) + [(spacing, spacing), (0, 0)]
    widened = jnp.pad(padded, widths)
    pieces = [widened[..., row_off * spacing: row_off * spacing + row_count, col_off * spacing: col_off * spacing + col_count, :]
              for row_off in range(3) for col_off in range(3)]
    stacked = jnp.concatenate(pieces, -1)
    flattened = stacked.reshape(-1, stacked.shape[-1])
    result = jnp.dot(flattened, weight, preferred_element_type=jnp.float32)
    return result.reshape(stacked.shape[:-1] + (weight.shape[1],))


def pad_rows(field, spacing):
    widths = [(0, 0)] * (field.ndim - 3) + [(spacing, spacing), (0, 0), (0, 0)]
    return jnp.pad(field, widths)


def lstm_update(gate_sums, memory):
    ingate, forget, candidate, outgate = jnp.split(gate_sums, 4, -1)
    memory = jax.nn.sigmoid(forget) * memory + jax.nn.sigmoid(ingate) * jnp.tanh(candidate)
    hidden = (jax.nn.sigmoid(outgate) * jnp.tanh(memory)).astype(jnp.bfloat16)
    return hidden, memory


def reference(frames, patch_weight, patch_bias, enc_weight, cell_weight, cell_bias, head_weight, out_weight, out_bias):
    results = []
    for sample_no in range(MB):
        patches = frames[sample_no].reshape(STEPS, NROWS, 2, COLS, 2 * CIN)
        upper = jnp.dot(patches[:, :, 0].reshape(-1, 2 * CIN), patch_weight[0], preferred_element_type=jnp.float32)
        lower = jnp.dot(patches[:, :, 1].reshape(-1, 2 * CIN), patch_weight[1], preferred_element_type=jnp.float32)
        projected = (upper + lower + patch_bias).reshape(STEPS, NROWS, COLS, C).astype(jnp.bfloat16)
        activated = jnp.maximum(projected, jnp.zeros((), jnp.bfloat16))
        encoded = (projected.astype(jnp.float32) + dilated(pad_rows(activated, 1), enc_weight, 1)).astype(jnp.bfloat16)
        sequence = encoded
        for layer_no in range(LAYERS):
            hidden = jnp.zeros((NROWS, COLS, C), jnp.bfloat16)
            memory = jnp.zeros((NROWS, COLS, C), jnp.float32)
            outputs = []
            for step_no in range(STEPS):
                joined = jnp.concatenate([sequence[step_no], hidden], -1)
                gate_sums = dilated(pad_rows(joined, 1), cell_weight[layer_no], 1) + cell_bias[layer_no]
                hidden, memory = lstm_update(gate_sums, memory)
                outputs.append(hidden)
            sequence = jnp.stack(outputs)
        residual_y = sequence.astype(jnp.float32)
        for layer_no, spacing in enumerate((1, 2, 4)):
            lifted = jnp.maximum(residual_y, 0.0).astype(jnp.bfloat16)
            residual_y = residual_y + dilated(pad_rows(lifted, spacing), head_weight[layer_no], spacing)
        rounded = residual_y.astype(jnp.bfloat16).reshape(-1, C)
        logits = (jnp.dot(rounded, out_weight, preferred_element_type=jnp.float32) + out_bias).astype(jnp.bfloat16)
        results.append(logits.reshape(STEPS, NROWS, COLS, BINS))
    return jnp.stack(results)
```

```python
import functools

import jax
import jax.numpy as jnp
from jax import lax
from jax.experimental import pallas as pl
from jax.experimental.pallas import tpu as pltpu
from jax.sharding import PartitionSpec as P

MESH = pl.DeviceIdType.MESH
BF16 = jnp.bfloat16
F32 = jnp.float32


def sigmoid(x):
    return 0.5 * jnp.tanh(0.5 * x) + 0.5


def shifted(field, by):
    cols = field.shape[1]
    wide = field.astype(F32)
    col = lax.broadcasted_iota(jnp.int32, field.shape, 1)
    left = jnp.where(col >= by, pltpu.roll(wide, by, 1), 0.0).astype(BF16)
    right = jnp.where(col < cols - by, pltpu.roll(wide, cols - by, 1), 0.0).astype(BF16)
    return left, field, right


def kernel(
    sections, spaces,
    frames, pw, pb, ew, cw_hbm, cb, hw,
    out,
    fr, cw, proj, ebox, enc, xbox, hbox, gbox, l1box, l2box, mem, resid, joined,
    fr_sem, cw_sem, e_recv, e_send, enc_send, x_recv, h_recv, u_send, g_recv,
    l1_recv, l1_send, l2_recv, l2_send,
):
    layer = lax.axis_index("section")
    place = lax.axis_index("space")
    last = sections - 1
    has_up = place > 0
    has_down = place < spaces - 1
    above = jnp.maximum(place - 1, 0)
    below = jnp.minimum(place + 1, spaces - 1)
    onward = jnp.minimum(layer + 1, last)
    steps, rows = fr.shape[0], fr.shape[1]
    cols, ch = proj.shape[1] // rows, proj.shape[2]
    cells = rows * cols

    def frame_copy(t):
        return pltpu.make_async_copy(frames.at[t], fr.at[t], fr_sem.at[t])

    weight_copy = pltpu.make_async_copy(cw_hbm, cw, cw_sem.at[0])
    for t in range(steps):
        frame_copy(t).start()
    weight_copy.start()

    barrier = pltpu.get_barrier_semaphore()
    for sec in range(sections):
        @pl.when(has_up)
        def _():
            pl.semaphore_signal(barrier, inc=1, device_id=(sec, above), device_id_type=MESH)

        @pl.when(has_down)
        def _():
            pl.semaphore_signal(barrier, inc=1, device_id=(sec, below), device_id_type=MESH)

        @pl.when(layer != sec)
        def _():
            pl.semaphore_signal(barrier, inc=1, device_id=(sec, place), device_id_type=MESH)

    @pl.when(jnp.logical_not(has_up))
    def _():
        for box, depth in ((ebox, 1), (xbox, 1), (hbox, 1), (gbox, 1), (l1box, 2), (l2box, 4)):
            box[:, 0:depth] = jnp.zeros((box.shape[0], depth, cols, ch), BF16)

    @pl.when(jnp.logical_not(has_down))
    def _():
        for box, depth in ((ebox, 1), (xbox, 1), (hbox, 1), (gbox, 1), (l1box, 2), (l2box, 4)):
            end = box.shape[1]
            box[:, end - depth:end] = jnp.zeros((box.shape[0], depth, cols, ch), BF16)

    def send(src, dst, s_sem, r_sem, sec, at):
        return pltpu.make_async_remote_copy(
            src_ref=src, dst_ref=dst, send_sem=s_sem, recv_sem=r_sem,
            device_id=(sec, at), device_id_type=MESH,
        )

    def edges(src, first, dst, depth, s_sem, s_at, r_sem, r_at, sec, go):
        end = dst.shape[0]
        up = send(src.at[pl.ds(first, depth)], dst.at[pl.ds(end - depth, depth)],
                  s_sem(s_at), r_sem(r_at + 1), sec, above)
        down = send(src.at[pl.ds(first + rows - depth, depth)], dst.at[pl.ds(0, depth)],
                    s_sem(s_at + 1), r_sem(r_at), sec, below)

        @pl.when(has_up)
        def _():
            go(up)

        @pl.when(has_down)
        def _():
            go(down)

    def start(copy):
        copy.start()

    def wait_sent(copy):
        copy.wait_send()

    def arrived(ref, sem):
        pltpu.make_async_copy(ref, ref, sem).wait()

    def edges_arrived(box, depth, sem, at):
        end = box.shape[0]

        @pl.when(has_up)
        def _():
            arrived(box.at[pl.ds(0, depth)], sem(at))

        @pl.when(has_down)
        def _():
            arrived(box.at[pl.ds(end - depth, depth)], sem(at + 1))

    def patch(a, b):
        return pw[a, b * ch:(b + 1) * ch, :]

    def ebox_edges(t, go):
        edges(ebox.at[t], 1, ebox.at[t], 1, lambda k: e_send.at[t, k], 0,
              lambda k: e_recv.at[t, k], 0, layer, go)

    def project(t):
        frame_copy(t).wait()
        fine = fr.shape[3]
        place_row = lax.broadcasted_iota(jnp.int32, (fine, fine), 0)
        place_col = lax.broadcasted_iota(jnp.int32, (fine, fine), 1)
        wanted = jnp.where(place_row < cols, 2 * place_row, 2 * place_row - (fine - 1))
        pick = jnp.where(place_col == wanted, 1.0, 0.0).astype(BF16)
        split = []
        for r in range(rows):
            pair = jnp.concatenate([fr[t, r, 0], fr[t, r, 1]], -1)
            both = jnp.dot(pick, pair, preferred_element_type=F32).astype(BF16)
            split.append(jnp.concatenate([both[:cols], both[cols:]], -1))
        weight = jnp.concatenate([patch(a, b) for b in range(2) for a in range(2)], 0)
        total = jnp.dot(jnp.concatenate(split, 0), weight, preferred_element_type=F32) + pb[...]
        rounded = total.astype(BF16)
        proj[t] = rounded
        ebox[t, pl.ds(1, rows)] = jnp.maximum(rounded, jnp.zeros((), BF16)).reshape(rows, cols, ch)

    project(0)
    present = 1 + jnp.where(has_up, 1, 0) + jnp.where(has_down, 1, 0)
    pl.semaphore_wait(barrier, sections * present - 1)
    ebox_edges(0, start)

    @pl.loop(1, steps)
    def _(t):
        project(t)
        ebox_edges(t, start)

    def conv(field, weight, by):
        parts = shifted(field, by)
        lhs = jnp.concatenate(
            [part[i * by:i * by + rows].reshape(cells, ch) for i in range(3) for part in parts], -1
        )
        return jnp.dot(lhs, weight, preferred_element_type=F32)

    def enc_out(t, go):
        slot = t * sections + layer
        edges(enc.at[t], 0, xbox.at[slot], 1, lambda k: enc_send.at[t, k], 0,
              lambda k: x_recv.at[slot, k], 0, 0, go)

    def enc_main(t):
        slot = t * sections + layer
        return send(enc.at[t], xbox.at[slot, pl.ds(1, rows)], enc_send.at[t, 2], x_recv.at[slot, 2], 0, place)

    @pl.loop(0, steps)
    def _(t):
        edges_arrived(ebox.at[t], 1, lambda k: e_recv.at[t, k], 0)
        result = proj[t].astype(F32) + conv(ebox[t], ew[...], 1)
        enc[t] = result.astype(BF16).reshape(rows, cols, ch)
        slot = t * sections + layer

        @pl.when(layer == 0)
        def _():
            pltpu.make_async_copy(enc.at[t], xbox.at[slot, pl.ds(1, rows)], x_recv.at[slot, 2]).start()

        @pl.when(layer != 0)
        def _():
            enc_main(t).start()

        enc_out(t, start)

    weight_copy.wait()

    def h_edges(slot, go):
        edges(hbox.at[slot], 1, hbox.at[slot], 1, lambda k: u_send.at[slot, k], 0,
              lambda k: h_recv.at[slot, k], 0, layer, go)

    def x_edges(slot, go):
        edges(hbox.at[slot], 1, xbox.at[slot], 1, lambda k: u_send.at[slot, k], 2,
              lambda k: x_recv.at[slot, k], 0, onward, go)

    def g_edges(t, m, go):
        slot = t * sections + m
        edges(hbox.at[slot], 1, gbox.at[t], 1, lambda k: u_send.at[slot, k], 2,
              lambda k: g_recv.at[t, k], 0, m, go)

    def x_main(slot):
        return send(hbox.at[slot, pl.ds(1, rows)], xbox.at[slot, pl.ds(1, rows)],
                    u_send.at[slot, 4], x_recv.at[slot, 2], onward, place)

    def g_main(t, m):
        slot = t * sections + m
        return send(hbox.at[slot, pl.ds(1, rows)], gbox.at[t, pl.ds(1, rows)],
                    u_send.at[slot, 4], g_recv.at[t, 2], m, place)

    def outgoing(t, m, go):
        slot = t * sections + m

        @pl.when(layer < last)
        def _():
            go(x_main(slot))
            x_edges(slot, go)

        @pl.when(layer == last)
        def _():
            @pl.when(m != last)
            def _():
                go(g_main(t, m))

            g_edges(t, m, go)

        @pl.when(t < steps - 1)
        def _():
            h_edges(slot, go)

    def unit(t, m, first):
        slot = t * sections + m
        arrived(xbox.at[slot, pl.ds(1, rows)], x_recv.at[slot, 2])
        edges_arrived(xbox.at[slot], 1, lambda k: x_recv.at[slot, k], 0)
        width = 2 * ch
        if first:
            parts = shifted(xbox[slot], 1)
            for j in range(3):
                joined[:, :, j * ch:(j + 1) * ch] = parts[j]
            lhs = jnp.concatenate(
                [joined[i:i + rows, :, 0:3 * ch].reshape(cells, 3 * ch) for i in range(3)], -1
            )
            weight = jnp.concatenate([cw[k * width:k * width + ch] for k in range(9)], 0)
        else:
            before = slot - sections
            edges_arrived(hbox.at[before], 1, lambda k: h_recv.at[before, k], 0)
            parts = shifted(xbox[slot], 1)
            for j in range(3):
                joined[:, :, j * width:j * width + ch] = parts[j]
            parts = shifted(hbox[before], 1)
            for j in range(3):
                joined[:, :, j * width + ch:(j + 1) * width] = parts[j]
            lhs = jnp.concatenate(
                [joined[i:i + rows].reshape(cells, 3 * width) for i in range(3)], -1
            )
            weight = cw[...]
        z = jnp.dot(lhs, weight, preferred_element_type=F32) + cb[...]
        new = sigmoid(z[:, :ch]) * jnp.tanh(z[:, 2 * ch:3 * ch])
        if not first:
            new = new + sigmoid(z[:, ch:2 * ch]) * mem[m]
        mem[m] = new
        hidden = (sigmoid(z[:, 3 * ch:]) * jnp.tanh(new)).astype(BF16)
        hbox[slot, pl.ds(1, rows)] = hidden.reshape(rows, cols, ch)

        @pl.when(jnp.logical_and(layer == last, m == last))
        def _():
            pltpu.make_async_copy(
                hbox.at[slot, pl.ds(1, rows)], gbox.at[t, pl.ds(1, rows)], g_recv.at[t, 2]
            ).start()

        outgoing(t, m, start)

    @pl.loop(0, sections)
    def _(m):
        unit(0, m, True)

    @pl.loop(1, steps)
    def _(t):
        @pl.loop(0, sections)
        def _(m):
            unit(t, m, False)

    def l1_edges(t, go):
        edges(l1box.at[t], 2, l1box.at[t], 2, lambda k: l1_send.at[t, k], 0,
              lambda k: l1_recv.at[t, k], 0, layer, go)

    def l2_edges(t, go):
        edges(l2box.at[t], 4, l2box.at[t], 4, lambda k: l2_send.at[t, k], 0,
              lambda k: l2_recv.at[t, k], 0, layer, go)

    zero = jnp.zeros((), BF16)

    @pl.loop(0, steps)
    def _(t):
        arrived(gbox.at[t, pl.ds(1, rows)], g_recv.at[t, 2])
        edges_arrived(gbox.at[t], 1, lambda k: g_recv.at[t, k], 0)
        base = gbox[t, pl.ds(1, rows)].reshape(cells, ch).astype(F32)
        y = base + conv(jnp.maximum(gbox[t], zero), hw[0], 1)
        resid[t] = y
        l1box[t, pl.ds(2, rows)] = jnp.maximum(y, 0.0).astype(BF16).reshape(rows, cols, ch)
        l1_edges(t, start)

    @pl.loop(0, steps)
    def _(t):
        edges_arrived(l1box.at[t], 2, lambda k: l1_recv.at[t, k], 0)
        y = resid[t] + conv(l1box[t], hw[1], 2)
        resid[t] = y
        l2box[t, pl.ds(4, rows)] = jnp.maximum(y, 0.0).astype(BF16).reshape(rows, cols, ch)
        l2_edges(t, start)

    @pl.loop(0, steps)
    def _(t):
        edges_arrived(l2box.at[t], 4, lambda k: l2_recv.at[t, k], 0)
        out[t] = (resid[t] + conv(l2box[t], hw[2], 4)).astype(BF16)

    @pl.loop(0, steps)
    def _(t):
        ebox_edges(t, wait_sent)
        enc_out(t, wait_sent)

        @pl.when(layer != 0)
        def _():
            enc_main(t).wait_send()

        l1_edges(t, wait_sent)
        l2_edges(t, wait_sent)

    @pl.loop(0, steps)
    def _(t):
        @pl.loop(0, sections)
        def _(m):
            outgoing(t, m, wait_sent)


def local(sections, spaces, frames, patch_weight, patch_bias, enc_weight, cell_weight,
          cell_bias, head_weight, out_weight, out_bias):
    _, steps, fine_rows, fine_cols, ch_in = frames.shape
    rows, cols = fine_rows // 2, fine_cols // 2
    ch = enc_weight.shape[1]
    cells = rows * cols
    slots = steps * sections
    vmem = pl.BlockSpec(memory_space=pltpu.VMEM)
    hbm = pl.BlockSpec(memory_space=pl.ANY)
    dma = pltpu.SemaphoreType.DMA
    rounded = pl.pallas_call(
        functools.partial(kernel, sections, spaces),
        out_shape=jax.ShapeDtypeStruct((steps, cells, ch), BF16),
        in_specs=[hbm, vmem, vmem, vmem, hbm, vmem, vmem],
        out_specs=vmem,
        scratch_shapes=[
            pltpu.VMEM((steps, rows, 2, fine_cols, ch_in), BF16),
            pltpu.VMEM(cell_weight.shape[1:], BF16),
            pltpu.VMEM((steps, cells, ch), BF16),
            pltpu.VMEM((steps, rows + 2, cols, ch), BF16),
            pltpu.VMEM((steps, rows, cols, ch), BF16),
            pltpu.VMEM((slots, rows + 2, cols, ch), BF16),
            pltpu.VMEM((slots, rows + 2, cols, ch), BF16),
            pltpu.VMEM((steps, rows + 2, cols, ch), BF16),
            pltpu.VMEM((steps, rows + 4, cols, ch), BF16),
            pltpu.VMEM((steps, rows + 8, cols, ch), BF16),
            pltpu.VMEM((sections, cells, ch), F32),
            pltpu.VMEM((steps, cells, ch), F32),
            pltpu.VMEM((rows + 2, cols, 6 * ch), BF16),
            dma((steps,)), dma((1,)),
            dma((steps, 2)), dma((steps, 2)), dma((steps, 3)),
            dma((slots, 3)), dma((slots, 2)), dma((slots, 5)), dma((steps, 3)),
            dma((steps, 2)), dma((steps, 2)), dma((steps, 2)), dma((steps, 2)),
        ],
        compiler_params=pltpu.CompilerParams(
            collective_id=0, has_side_effects=True, vmem_limit_bytes=48 * 1024 * 1024
        ),
        name="nowcast",
    )(
        frames.reshape(steps, rows, 2, fine_cols, ch_in),
        patch_weight,
        patch_bias.reshape(1, ch),
        enc_weight,
        cell_weight[0],
        cell_bias,
        head_weight,
    )
    logits = jnp.dot(rounded.reshape(steps * cells, ch), out_weight, preferred_element_type=F32)
    logits = (logits + out_bias).astype(BF16)
    return logits.reshape(1, steps, rows, cols, out_weight.shape[1])


def solution(mesh):
    placed = (
        P("section", None, "space", None, None),
        P(), P(), P(),
        P("section", None, None),
        P("section", None),
        P(), P(), P(),
    )
    return jax.shard_map(
        functools.partial(local, mesh.shape["section"], mesh.shape["space"]),
        mesh=mesh,
        in_specs=placed,
        out_specs=P("section", None, "space", None, None),
        check_vma=False,
    )
```

```python
import functools

import jax
import jax.numpy as jnp
from jax import lax
from jax.experimental import pallas as pl
from jax.experimental.pallas import tpu as pltpu
from jax.sharding import PartitionSpec as P

MESH = pl.DeviceIdType.MESH
BF16 = jnp.bfloat16
F32 = jnp.float32


def sigmoid(x):
    return 0.5 * jnp.tanh(0.5 * x) + 0.5


def shifted(field, by):
    cols = field.shape[1]
    wide = field.astype(F32)
    col = lax.broadcasted_iota(jnp.int32, field.shape, 1)
    left = jnp.where(col >= by, pltpu.roll(wide, by, 1), 0.0).astype(BF16)
    right = jnp.where(col < cols - by, pltpu.roll(wide, cols - by, 1), 0.0).astype(BF16)
    return left, field, right


def kernel(
    sections, spaces,
    frames, pw_hbm, pb_hbm, ew_hbm, cw_hbm, cb_hbm, hw_hbm,
    out_hbm,
    fr, pw, pb, ew, cw, cb, hw, out, proj, ebox, enc, xbox, hbox, gbox, l1box, l2box, mem, resid, joined,
    fr_sem, w_sem, out_sem, e_recv, e_send, enc_send, x_recv, h_recv, u_send, g_recv,
    l1_recv, l1_send, l2_recv, l2_send,
):
    layer = lax.axis_index("section")
    place = lax.axis_index("space")
    last = sections - 1
    has_up = place > 0
    has_down = place < spaces - 1
    above = jnp.maximum(place - 1, 0)
    below = jnp.minimum(place + 1, spaces - 1)
    onward = jnp.minimum(layer + 1, last)
    steps, rows = fr.shape[0], fr.shape[1]
    cols, ch = proj.shape[1] // rows, proj.shape[2]
    cells = rows * cols

    def frame_copy(t):
        return pltpu.make_async_copy(frames.at[t], fr.at[t], fr_sem.at[t])

    pairs = ((pw_hbm, pw), (pb_hbm, pb), (ew_hbm, ew), (cw_hbm, cw), (cb_hbm, cb), (hw_hbm, hw))
    load_pw, load_pb, load_ew, load_cw, load_cb, load_hw = [
        pltpu.make_async_copy(src, dst, w_sem.at[k]) for k, (src, dst) in enumerate(pairs)
    ]
    load_pw.start()
    load_pb.start()
    for t in range(steps):
        frame_copy(t).start()
    for load in (load_ew, load_cw, load_cb, load_hw):
        load.start()

    barrier = pltpu.get_barrier_semaphore()
    for sec in range(sections):
        @pl.when(has_up)
        def _():
            pl.semaphore_signal(barrier, inc=1, device_id=(sec, above), device_id_type=MESH)

        @pl.when(has_down)
        def _():
            pl.semaphore_signal(barrier, inc=1, device_id=(sec, below), device_id_type=MESH)

        @pl.when(layer != sec)
        def _():
            pl.semaphore_signal(barrier, inc=1, device_id=(sec, place), device_id_type=MESH)

    @pl.when(jnp.logical_not(has_up))
    def _():
        for box, depth in ((ebox, 1), (xbox, 1), (hbox, 1), (gbox, 1), (l1box, 2), (l2box, 4)):
            box[:, 0:depth] = jnp.zeros((box.shape[0], depth, cols, ch), BF16)

    @pl.when(jnp.logical_not(has_down))
    def _():
        for box, depth in ((ebox, 1), (xbox, 1), (hbox, 1), (gbox, 1), (l1box, 2), (l2box, 4)):
            end = box.shape[1]
            box[:, end - depth:end] = jnp.zeros((box.shape[0], depth, cols, ch), BF16)

    def send(src, dst, s_sem, r_sem, sec, at):
        return pltpu.make_async_remote_copy(
            src_ref=src, dst_ref=dst, send_sem=s_sem, recv_sem=r_sem,
            device_id=(sec, at), device_id_type=MESH,
        )

    def edges(src, first, dst, depth, s_sem, s_at, r_sem, r_at, sec, go):
        end = dst.shape[0]
        up = send(src.at[pl.ds(first, depth)], dst.at[pl.ds(end - depth, depth)],
                  s_sem(s_at), r_sem(r_at + 1), sec, above)
        down = send(src.at[pl.ds(first + rows - depth, depth)], dst.at[pl.ds(0, depth)],
                    s_sem(s_at + 1), r_sem(r_at), sec, below)

        @pl.when(has_up)
        def _():
            go(up)

        @pl.when(has_down)
        def _():
            go(down)

    def start(copy):
        copy.start()

    def wait_sent(copy):
        copy.wait_send()

    def arrived(ref, sem):
        pltpu.make_async_copy(ref, ref, sem).wait()

    def edges_arrived(box, depth, sem, at):
        end = box.shape[0]

        @pl.when(has_up)
        def _():
            arrived(box.at[pl.ds(0, depth)], sem(at))

        @pl.when(has_down)
        def _():
            arrived(box.at[pl.ds(end - depth, depth)], sem(at + 1))

    def patch(a, b):
        return pw[a, b * ch:(b + 1) * ch, :]

    def ebox_edges(t, go):
        edges(ebox.at[t], 1, ebox.at[t], 1, lambda k: e_send.at[t, k], 0,
              lambda k: e_recv.at[t, k], 0, layer, go)

    def project(t):
        frame_copy(t).wait()
        fine = fr.shape[3]
        place_row = lax.broadcasted_iota(jnp.int32, (fine, fine), 0)
        place_col = lax.broadcasted_iota(jnp.int32, (fine, fine), 1)
        wanted = jnp.where(place_row < cols, 2 * place_row, 2 * place_row - (fine - 1))
        pick = jnp.where(place_col == wanted, 1.0, 0.0).astype(BF16)
        split = []
        for r in range(rows):
            pair = jnp.concatenate([fr[t, r, 0], fr[t, r, 1]], -1)
            both = jnp.dot(pick, pair, preferred_element_type=F32).astype(BF16)
            split.append(jnp.concatenate([both[:cols], both[cols:]], -1))
        weight = jnp.concatenate([patch(a, b) for b in range(2) for a in range(2)], 0)
        total = jnp.dot(jnp.concatenate(split, 0), weight, preferred_element_type=F32) + pb[...]
        rounded = total.astype(BF16)
        proj[t] = rounded
        ebox[t, pl.ds(1, rows)] = jnp.maximum(rounded, jnp.zeros((), BF16)).reshape(rows, cols, ch)

    load_pw.wait()
    load_pb.wait()
    project(0)
    present = 1 + jnp.where(has_up, 1, 0) + jnp.where(has_down, 1, 0)
    pl.semaphore_wait(barrier, sections * present - 1)
    ebox_edges(0, start)

    @pl.loop(1, steps)
    def _(t):
        project(t)
        ebox_edges(t, start)

    def conv(field, weight, by):
        parts = shifted(field, by)
        lhs = jnp.concatenate(
            [part[i * by:i * by + rows].reshape(cells, ch) for i in range(3) for part in parts], -1
        )
        return jnp.dot(lhs, weight, preferred_element_type=F32)

    load_ew.wait()

    def enc_out(t, go):
        slot = t * sections + layer
        edges(enc.at[t], 0, xbox.at[slot], 1, lambda k: enc_send.at[t, k], 0,
              lambda k: x_recv.at[slot, k], 0, 0, go)

    def enc_main(t):
        slot = t * sections + layer
        return send(enc.at[t], xbox.at[slot, pl.ds(1, rows)], enc_send.at[t, 2], x_recv.at[slot, 2], 0, place)

    @pl.loop(0, steps)
    def _(t):
        edges_arrived(ebox.at[t], 1, lambda k: e_recv.at[t, k], 0)
        result = proj[t].astype(F32) + conv(ebox[t], ew[...], 1)
        enc[t] = result.astype(BF16).reshape(rows, cols, ch)
        slot = t * sections + layer

        @pl.when(layer == 0)
        def _():
            pltpu.make_async_copy(enc.at[t], xbox.at[slot, pl.ds(1, rows)], x_recv.at[slot, 2]).start()

        @pl.when(layer != 0)
        def _():
            enc_main(t).start()

        enc_out(t, start)

    load_cw.wait()
    load_cb.wait()

    def h_edges(slot, go):
        edges(hbox.at[slot], 1, hbox.at[slot], 1, lambda k: u_send.at[slot, k], 0,
              lambda k: h_recv.at[slot, k], 0, layer, go)

    def x_edges(slot, go):
        edges(hbox.at[slot], 1, xbox.at[slot], 1, lambda k: u_send.at[slot, k], 2,
              lambda k: x_recv.at[slot, k], 0, onward, go)

    def g_edges(t, m, go):
        slot = t * sections + m
        edges(hbox.at[slot], 1, gbox.at[t], 1, lambda k: u_send.at[slot, k], 2,
              lambda k: g_recv.at[t, k], 0, m, go)

    def x_main(slot):
        return send(hbox.at[slot, pl.ds(1, rows)], xbox.at[slot, pl.ds(1, rows)],
                    u_send.at[slot, 4], x_recv.at[slot, 2], onward, place)

    def g_main(t, m):
        slot = t * sections + m
        return send(hbox.at[slot, pl.ds(1, rows)], gbox.at[t, pl.ds(1, rows)],
                    u_send.at[slot, 4], g_recv.at[t, 2], m, place)

    def outgoing(t, m, go):
        slot = t * sections + m

        @pl.when(layer < last)
        def _():
            go(x_main(slot))
            x_edges(slot, go)

        @pl.when(layer == last)
        def _():
            @pl.when(m != last)
            def _():
                go(g_main(t, m))

            g_edges(t, m, go)

        @pl.when(t < steps - 1)
        def _():
            h_edges(slot, go)

    def unit(t, m, first):
        slot = t * sections + m
        arrived(xbox.at[slot, pl.ds(1, rows)], x_recv.at[slot, 2])
        edges_arrived(xbox.at[slot], 1, lambda k: x_recv.at[slot, k], 0)
        width = 2 * ch
        if first:
            parts = shifted(xbox[slot], 1)
            for j in range(3):
                joined[:, :, j * ch:(j + 1) * ch] = parts[j]
            lhs = jnp.concatenate(
                [joined[i:i + rows, :, 0:3 * ch].reshape(cells, 3 * ch) for i in range(3)], -1
            )
            weight = jnp.concatenate([cw[k * width:k * width + ch] for k in range(9)], 0)
        else:
            before = slot - sections
            edges_arrived(hbox.at[before], 1, lambda k: h_recv.at[before, k], 0)
            parts = shifted(xbox[slot], 1)
            for j in range(3):
                joined[:, :, j * width:j * width + ch] = parts[j]
            parts = shifted(hbox[before], 1)
            for j in range(3):
                joined[:, :, j * width + ch:(j + 1) * width] = parts[j]
            lhs = jnp.concatenate(
                [joined[i:i + rows].reshape(cells, 3 * width) for i in range(3)], -1
            )
            weight = cw[...]
        z = jnp.dot(lhs, weight, preferred_element_type=F32) + cb[...]
        new = sigmoid(z[:, :ch]) * jnp.tanh(z[:, 2 * ch:3 * ch])
        if not first:
            new = new + sigmoid(z[:, ch:2 * ch]) * mem[m]
        mem[m] = new
        hidden = (sigmoid(z[:, 3 * ch:]) * jnp.tanh(new)).astype(BF16)
        hbox[slot, pl.ds(1, rows)] = hidden.reshape(rows, cols, ch)

        @pl.when(jnp.logical_and(layer == last, m == last))
        def _():
            pltpu.make_async_copy(
                hbox.at[slot, pl.ds(1, rows)], gbox.at[t, pl.ds(1, rows)], g_recv.at[t, 2]
            ).start()

        outgoing(t, m, start)

    @pl.loop(0, sections)
    def _(m):
        unit(0, m, True)

    @pl.loop(1, steps)
    def _(t):
        @pl.loop(0, sections)
        def _(m):
            unit(t, m, False)

    def out_copy(t):
        return pltpu.make_async_copy(out.at[t], out_hbm.at[t], out_sem.at[t])

    load_hw.wait()

    def l1_edges(t, go):
        edges(l1box.at[t], 2, l1box.at[t], 2, lambda k: l1_send.at[t, k], 0,
              lambda k: l1_recv.at[t, k], 0, layer, go)

    def l2_edges(t, go):
        edges(l2box.at[t], 4, l2box.at[t], 4, lambda k: l2_send.at[t, k], 0,
              lambda k: l2_recv.at[t, k], 0, layer, go)

    zero = jnp.zeros((), BF16)

    @pl.loop(0, steps)
    def _(t):
        arrived(gbox.at[t, pl.ds(1, rows)], g_recv.at[t, 2])
        edges_arrived(gbox.at[t], 1, lambda k: g_recv.at[t, k], 0)
        base = gbox[t, pl.ds(1, rows)].reshape(cells, ch).astype(F32)
        y = base + conv(jnp.maximum(gbox[t], zero), hw[0], 1)
        resid[t] = y
        l1box[t, pl.ds(2, rows)] = jnp.maximum(y, 0.0).astype(BF16).reshape(rows, cols, ch)
        l1_edges(t, start)

    @pl.loop(0, steps)
    def _(t):
        edges_arrived(l1box.at[t], 2, lambda k: l1_recv.at[t, k], 0)
        y = resid[t] + conv(l1box[t], hw[1], 2)
        resid[t] = y
        l2box[t, pl.ds(4, rows)] = jnp.maximum(y, 0.0).astype(BF16).reshape(rows, cols, ch)
        l2_edges(t, start)

    @pl.loop(0, steps)
    def _(t):
        edges_arrived(l2box.at[t], 4, lambda k: l2_recv.at[t, k], 0)
        out[t] = (resid[t] + conv(l2box[t], hw[2], 4)).astype(BF16)
        out_copy(t).start()

    for t in range(steps):
        out_copy(t).wait()

    @pl.loop(0, steps)
    def _(t):
        ebox_edges(t, wait_sent)
        enc_out(t, wait_sent)

        @pl.when(layer != 0)
        def _():
            enc_main(t).wait_send()

        l1_edges(t, wait_sent)
        l2_edges(t, wait_sent)

    @pl.loop(0, steps)
    def _(t):
        @pl.loop(0, sections)
        def _(m):
            outgoing(t, m, wait_sent)


def local(sections, spaces, frames, patch_weight, patch_bias, enc_weight, cell_weight,
          cell_bias, head_weight, out_weight, out_bias):
    _, steps, fine_rows, fine_cols, ch_in = frames.shape
    rows, cols = fine_rows // 2, fine_cols // 2
    ch = enc_weight.shape[1]
    cells = rows * cols
    slots = steps * sections
    hbm = pl.BlockSpec(memory_space=pl.ANY)
    dma = pltpu.SemaphoreType.DMA
    rounded = pl.pallas_call(
        functools.partial(kernel, sections, spaces),
        out_shape=jax.ShapeDtypeStruct((steps, cells, ch), BF16),
        in_specs=[hbm] * 7,
        out_specs=hbm,
        scratch_shapes=[
            pltpu.VMEM((steps, rows, 2, fine_cols, ch_in), BF16),
            pltpu.VMEM(patch_weight.shape, BF16),
            pltpu.VMEM((1, ch), F32),
            pltpu.VMEM(enc_weight.shape, BF16),
            pltpu.VMEM(cell_weight.shape[1:], BF16),
            pltpu.VMEM(cell_bias.shape, F32),
            pltpu.VMEM(head_weight.shape, BF16),
            pltpu.VMEM((steps, cells, ch), BF16),
            pltpu.VMEM((steps, cells, ch), BF16),
            pltpu.VMEM((steps, rows + 2, cols, ch), BF16),
            pltpu.VMEM((steps, rows, cols, ch), BF16),
            pltpu.VMEM((slots, rows + 2, cols, ch), BF16),
            pltpu.VMEM((slots, rows + 2, cols, ch), BF16),
            pltpu.VMEM((steps, rows + 2, cols, ch), BF16),
            pltpu.VMEM((steps, rows + 4, cols, ch), BF16),
            pltpu.VMEM((steps, rows + 8, cols, ch), BF16),
            pltpu.VMEM((sections, cells, ch), F32),
            pltpu.VMEM((steps, cells, ch), F32),
            pltpu.VMEM((rows + 2, cols, 6 * ch), BF16),
            dma((steps,)), dma((6,)), dma((steps,)),
            dma((steps, 2)), dma((steps, 2)), dma((steps, 3)),
            dma((slots, 3)), dma((slots, 2)), dma((slots, 5)), dma((steps, 3)),
            dma((steps, 2)), dma((steps, 2)), dma((steps, 2)), dma((steps, 2)),
        ],
        compiler_params=pltpu.CompilerParams(
            collective_id=0, has_side_effects=True, vmem_limit_bytes=56 * 1024 * 1024
        ),
        name="nowcast",
    )(
        frames.reshape(steps, rows, 2, fine_cols, ch_in),
        patch_weight,
        patch_bias.reshape(1, ch),
        enc_weight,
        cell_weight[0],
        cell_bias,
        head_weight,
    )
    logits = jnp.dot(rounded.reshape(steps * cells, ch), out_weight, preferred_element_type=F32)
    logits = (logits + out_bias).astype(BF16)
    return logits.reshape(1, steps, rows, cols, out_weight.shape[1])


def solution(mesh):
    placed = (
        P("section", None, "space", None, None),
        P(), P(), P(),
        P("section", None, None),
        P("section", None),
        P(), P(), P(),
    )
    return jax.shard_map(
        functools.partial(local, mesh.shape["section"], mesh.shape["space"]),
        mesh=mesh,
        in_specs=placed,
        out_specs=P("section", None, "space", None, None),
        check_vma=False,
    )
```

```python
import functools

import jax
import jax.numpy as jnp
from jax import lax
from jax.experimental import pallas as pl
from jax.experimental.pallas import tpu as pltpu
from jax.sharding import PartitionSpec as P

MESH = pl.DeviceIdType.MESH
BF16 = jnp.bfloat16
F32 = jnp.float32


def sigmoid(x):
    return 0.5 * jnp.tanh(0.5 * x) + 0.5


def shifted(field, by):
    cols = field.shape[1]
    wide = field.astype(F32)
    col = lax.broadcasted_iota(jnp.int32, field.shape, 1)
    left = jnp.where(col >= by, pltpu.roll(wide, by, 1), 0.0).astype(BF16)
    right = jnp.where(col < cols - by, pltpu.roll(wide, cols - by, 1), 0.0).astype(BF16)
    return left, field, right


def kernel(
    sections, spaces,
    frames, pw_hbm, pb_hbm, ew_hbm, cw_hbm, cb_hbm, hw_hbm,
    out_hbm,
    fr, pw, pb, ew, cw, cb, hw, out, proj, ebox, enc, xbox, hbox, gbox, l1box, l2box, mem, resid, joined,
    fr_sem, w_sem, out_sem, e_recv, e_send, enc_send, x_recv, h_recv, u_send, g_recv,
    l1_recv, l1_send, l2_recv, l2_send,
):
    layer = lax.axis_index("section")
    place = lax.axis_index("space")
    last = sections - 1
    has_up = place > 0
    has_down = place < spaces - 1
    above = jnp.maximum(place - 1, 0)
    below = jnp.minimum(place + 1, spaces - 1)
    onward = jnp.minimum(layer + 1, last)
    steps, rows = fr.shape[0], fr.shape[1]
    cols, ch = proj.shape[1] // rows, proj.shape[2]
    cells = rows * cols

    def frame_copy(t):
        return pltpu.make_async_copy(frames.at[t], fr.at[t], fr_sem.at[t])

    pairs = ((pw_hbm, pw), (pb_hbm, pb), (ew_hbm, ew), (cw_hbm, cw), (cb_hbm, cb), (hw_hbm, hw))
    load_pw, load_pb, load_ew, load_cw, load_cb, load_hw = [
        pltpu.make_async_copy(src, dst, w_sem.at[k]) for k, (src, dst) in enumerate(pairs)
    ]
    load_pw.start()
    load_pb.start()
    for t in range(steps):
        frame_copy(t).start()
    for load in (load_ew, load_cw, load_cb, load_hw):
        load.start()

    barrier = pltpu.get_barrier_semaphore()
    for sec in range(sections):
        @pl.when(has_up)
        def _():
            pl.semaphore_signal(barrier, inc=1, device_id=(sec, above), device_id_type=MESH)

        @pl.when(has_down)
        def _():
            pl.semaphore_signal(barrier, inc=1, device_id=(sec, below), device_id_type=MESH)

        @pl.when(layer != sec)
        def _():
            pl.semaphore_signal(barrier, inc=1, device_id=(sec, place), device_id_type=MESH)

    @pl.when(jnp.logical_not(has_up))
    def _():
        for box, depth in ((ebox, 1), (xbox, 1), (hbox, 1), (gbox, 1), (l1box, 2), (l2box, 4)):
            box[:, 0:depth] = jnp.zeros((box.shape[0], depth, cols, ch), BF16)

    @pl.when(jnp.logical_not(has_down))
    def _():
        for box, depth in ((ebox, 1), (xbox, 1), (hbox, 1), (gbox, 1), (l1box, 2), (l2box, 4)):
            end = box.shape[1]
            box[:, end - depth:end] = jnp.zeros((box.shape[0], depth, cols, ch), BF16)

    def send(src, dst, s_sem, r_sem, sec, at):
        return pltpu.make_async_remote_copy(
            src_ref=src, dst_ref=dst, send_sem=s_sem, recv_sem=r_sem,
            device_id=(sec, at), device_id_type=MESH,
        )

    def edges(src, first, dst, depth, s_sem, s_at, r_sem, r_at, sec, go):
        end = dst.shape[0]
        up = send(src.at[pl.ds(first, depth)], dst.at[pl.ds(end - depth, depth)],
                  s_sem(s_at), r_sem(r_at + 1), sec, above)
        down = send(src.at[pl.ds(first + rows - depth, depth)], dst.at[pl.ds(0, depth)],
                    s_sem(s_at + 1), r_sem(r_at), sec, below)

        @pl.when(has_up)
        def _():
            go(up)

        @pl.when(has_down)
        def _():
            go(down)

    def start(copy):
        copy.start()

    def wait_sent(copy):
        copy.wait_send()

    def arrived(ref, sem):
        pltpu.make_async_copy(ref, ref, sem).wait()

    def edges_arrived(box, depth, sem, at):
        end = box.shape[0]

        @pl.when(has_up)
        def _():
            arrived(box.at[pl.ds(0, depth)], sem(at))

        @pl.when(has_down)
        def _():
            arrived(box.at[pl.ds(end - depth, depth)], sem(at + 1))

    def patch(a, b):
        return pw[a, b * ch:(b + 1) * ch, :]

    def ebox_edges(t, go):
        edges(ebox.at[t], 1, ebox.at[t], 1, lambda k: e_send.at[t, k], 0,
              lambda k: e_recv.at[t, k], 0, layer, go)

    def project(t):
        frame_copy(t).wait()
        fine = fr.shape[3]
        place_row = lax.broadcasted_iota(jnp.int32, (fine, fine), 0)
        place_col = lax.broadcasted_iota(jnp.int32, (fine, fine), 1)
        wanted = jnp.where(place_row < cols, 2 * place_row, 2 * place_row - (fine - 1))
        pick = jnp.where(place_col == wanted, 1.0, 0.0).astype(BF16)
        split = []
        for r in range(rows):
            pair = jnp.concatenate([fr[t, r, 0], fr[t, r, 1]], -1)
            both = jnp.dot(pick, pair, preferred_element_type=F32).astype(BF16)
            split.append(jnp.concatenate([both[:cols], both[cols:]], -1))
        weight = jnp.concatenate([patch(a, b) for b in range(2) for a in range(2)], 0)
        total = jnp.dot(jnp.concatenate(split, 0), weight, preferred_element_type=F32) + pb[...]
        rounded = total.astype(BF16)
        proj[t] = rounded
        ebox[t, pl.ds(1, rows)] = jnp.maximum(rounded, jnp.zeros((), BF16)).reshape(rows, cols, ch)

    load_pw.wait()
    load_pb.wait()
    project(0)
    present = 1 + jnp.where(has_up, 1, 0) + jnp.where(has_down, 1, 0)
    pl.semaphore_wait(barrier, sections * present - 1)
    ebox_edges(0, start)

    @pl.loop(1, steps)
    def _(t):
        project(t)
        ebox_edges(t, start)

    def conv(field, weight, by):
        parts = shifted(field, by)
        lhs = jnp.concatenate(
            [part[i * by:i * by + rows].reshape(cells, ch) for i in range(3) for part in parts], -1
        )
        return jnp.dot(lhs, weight, preferred_element_type=F32)

    load_ew.wait()

    def enc_out(t, go):
        slot = t * sections + layer
        edges(enc.at[t], 0, xbox.at[slot], 1, lambda k: enc_send.at[t, k], 0,
              lambda k: x_recv.at[slot, k], 0, 0, go)

    def enc_main(t):
        slot = t * sections + layer
        return send(enc.at[t], xbox.at[slot, pl.ds(1, rows)], enc_send.at[t, 2], x_recv.at[slot, 2], 0, place)

    @pl.loop(0, steps)
    def _(t):
        edges_arrived(ebox.at[t], 1, lambda k: e_recv.at[t, k], 0)
        result = proj[t].astype(F32) + conv(ebox[t], ew[...], 1)
        enc[t] = result.astype(BF16).reshape(rows, cols, ch)
        slot = t * sections + layer

        @pl.when(layer == 0)
        def _():
            pltpu.make_async_copy(enc.at[t], xbox.at[slot, pl.ds(1, rows)], x_recv.at[slot, 2]).start()

        @pl.when(layer != 0)
        def _():
            enc_main(t).start()

        enc_out(t, start)

    load_cw.wait()
    load_cb.wait()
    load_hw.wait()

    def h_edges(slot, go):
        edges(hbox.at[slot], 1, hbox.at[slot], 1, lambda k: u_send.at[slot, k], 0,
              lambda k: h_recv.at[slot, k], 0, layer, go)

    def x_edges(slot, go):
        edges(hbox.at[slot], 1, xbox.at[slot], 1, lambda k: u_send.at[slot, k], 2,
              lambda k: x_recv.at[slot, k], 0, onward, go)

    def g_edges(t, m, go):
        slot = t * sections + m
        edges(hbox.at[slot], 1, gbox.at[t], 1, lambda k: u_send.at[slot, k], 2,
              lambda k: g_recv.at[t, k], 0, m, go)

    def x_main(slot):
        return send(hbox.at[slot, pl.ds(1, rows)], xbox.at[slot, pl.ds(1, rows)],
                    u_send.at[slot, 4], x_recv.at[slot, 2], onward, place)

    def g_main(t, m):
        slot = t * sections + m
        return send(hbox.at[slot, pl.ds(1, rows)], gbox.at[t, pl.ds(1, rows)],
                    u_send.at[slot, 4], g_recv.at[t, 2], m, place)

    def outgoing(t, m, go):
        slot = t * sections + m

        @pl.when(layer < last)
        def _():
            go(x_main(slot))
            x_edges(slot, go)

        @pl.when(layer == last)
        def _():
            @pl.when(m != last)
            def _():
                go(g_main(t, m))

            g_edges(t, m, go)

        @pl.when(t < steps - 1)
        def _():
            h_edges(slot, go)

    def unit(t, m, first):
        slot = t * sections + m
        arrived(xbox.at[slot, pl.ds(1, rows)], x_recv.at[slot, 2])
        edges_arrived(xbox.at[slot], 1, lambda k: x_recv.at[slot, k], 0)
        width = 2 * ch
        if first:
            parts = shifted(xbox[slot], 1)
            for j in range(3):
                joined[:, :, j * ch:(j + 1) * ch] = parts[j]
            lhs = jnp.concatenate(
                [joined[i:i + rows, :, 0:3 * ch].reshape(cells, 3 * ch) for i in range(3)], -1
            )
            weight = jnp.concatenate([cw[k * width:k * width + ch] for k in range(9)], 0)
        else:
            before = slot - sections
            edges_arrived(hbox.at[before], 1, lambda k: h_recv.at[before, k], 0)
            parts = shifted(xbox[slot], 1)
            for j in range(3):
                joined[:, :, j * width:j * width + ch] = parts[j]
            parts = shifted(hbox[before], 1)
            for j in range(3):
                joined[:, :, j * width + ch:(j + 1) * width] = parts[j]
            lhs = jnp.concatenate(
                [joined[i:i + rows].reshape(cells, 3 * width) for i in range(3)], -1
            )
            weight = cw[...]
        z = jnp.dot(lhs, weight, preferred_element_type=F32) + cb[...]
        new = sigmoid(z[:, :ch]) * jnp.tanh(z[:, 2 * ch:3 * ch])
        if not first:
            new = new + sigmoid(z[:, ch:2 * ch]) * mem[m]
        mem[m] = new
        hidden = (sigmoid(z[:, 3 * ch:]) * jnp.tanh(new)).astype(BF16)
        hbox[slot, pl.ds(1, rows)] = hidden.reshape(rows, cols, ch)

        @pl.when(jnp.logical_and(layer == last, m == last))
        def _():
            pltpu.make_async_copy(
                hbox.at[slot, pl.ds(1, rows)], gbox.at[t, pl.ds(1, rows)], g_recv.at[t, 2]
            ).start()

        outgoing(t, m, start)

    def out_copy(t):
        return pltpu.make_async_copy(out.at[t], out_hbm.at[t], out_sem.at[t])

    def l1_edges(t, go):
        edges(l1box.at[t], 2, l1box.at[t], 2, lambda k: l1_send.at[t, k], 0,
              lambda k: l1_recv.at[t, k], 0, layer, go)

    def l2_edges(t, go):
        edges(l2box.at[t], 4, l2box.at[t], 4, lambda k: l2_send.at[t, k], 0,
              lambda k: l2_recv.at[t, k], 0, layer, go)

    zero = jnp.zeros((), BF16)

    def head_first(t):
        arrived(gbox.at[t, pl.ds(1, rows)], g_recv.at[t, 2])
        edges_arrived(gbox.at[t], 1, lambda k: g_recv.at[t, k], 0)
        base = gbox[t, pl.ds(1, rows)].reshape(cells, ch).astype(F32)
        y = base + conv(jnp.maximum(gbox[t], zero), hw[0], 1)
        resid[t] = y
        l1box[t, pl.ds(2, rows)] = jnp.maximum(y, 0.0).astype(BF16).reshape(rows, cols, ch)
        l1_edges(t, start)

    def head_second(t):
        edges_arrived(l1box.at[t], 2, lambda k: l1_recv.at[t, k], 0)
        y = resid[t] + conv(l1box[t], hw[1], 2)
        resid[t] = y
        l2box[t, pl.ds(4, rows)] = jnp.maximum(y, 0.0).astype(BF16).reshape(rows, cols, ch)
        l2_edges(t, start)

    def head_third(t):
        edges_arrived(l2box.at[t], 4, lambda k: l2_recv.at[t, k], 0)
        out[t] = (resid[t] + conv(l2box[t], hw[2], 4)).astype(BF16)
        out_copy(t).start()

    @pl.loop(0, sections)
    def _(m):
        unit(0, m, True)

    @pl.loop(1, steps)
    def _(t):
        @pl.loop(0, sections)
        def _(m):
            unit(t, m, False)

            for at, stage in ((1, head_first), (2, head_second), (3, head_third)):
                @pl.when(jnp.logical_and(layer == last, m == min(at, sections - 1)))
                def _():
                    stage(t - 1)

    @pl.loop(0, steps)
    def _(t):
        @pl.when(jnp.logical_or(layer != last, t == steps - 1))
        def _():
            head_first(t)
            head_second(t)
            head_third(t)

    for t in range(steps):
        out_copy(t).wait()

    @pl.loop(0, steps)
    def _(t):
        ebox_edges(t, wait_sent)
        enc_out(t, wait_sent)

        @pl.when(layer != 0)
        def _():
            enc_main(t).wait_send()

        l1_edges(t, wait_sent)
        l2_edges(t, wait_sent)

    @pl.loop(0, steps)
    def _(t):
        @pl.loop(0, sections)
        def _(m):
            outgoing(t, m, wait_sent)


def local(sections, spaces, frames, patch_weight, patch_bias, enc_weight, cell_weight,
          cell_bias, head_weight, out_weight, out_bias):
    _, steps, fine_rows, fine_cols, ch_in = frames.shape
    rows, cols = fine_rows // 2, fine_cols // 2
    ch = enc_weight.shape[1]
    cells = rows * cols
    slots = steps * sections
    hbm = pl.BlockSpec(memory_space=pl.ANY)
    dma = pltpu.SemaphoreType.DMA
    rounded = pl.pallas_call(
        functools.partial(kernel, sections, spaces),
        out_shape=jax.ShapeDtypeStruct((steps, cells, ch), BF16),
        in_specs=[hbm] * 7,
        out_specs=hbm,
        scratch_shapes=[
            pltpu.VMEM((steps, rows, 2, fine_cols, ch_in), BF16),
            pltpu.VMEM(patch_weight.shape, BF16),
            pltpu.VMEM((1, ch), F32),
            pltpu.VMEM(enc_weight.shape, BF16),
            pltpu.VMEM(cell_weight.shape[1:], BF16),
            pltpu.VMEM(cell_bias.shape, F32),
            pltpu.VMEM(head_weight.shape, BF16),
            pltpu.VMEM((steps, cells, ch), BF16),
            pltpu.VMEM((steps, cells, ch), BF16),
            pltpu.VMEM((steps, rows + 2, cols, ch), BF16),
            pltpu.VMEM((steps, rows, cols, ch), BF16),
            pltpu.VMEM((slots, rows + 2, cols, ch), BF16),
            pltpu.VMEM((slots, rows + 2, cols, ch), BF16),
            pltpu.VMEM((steps, rows + 2, cols, ch), BF16),
            pltpu.VMEM((steps, rows + 4, cols, ch), BF16),
            pltpu.VMEM((steps, rows + 8, cols, ch), BF16),
            pltpu.VMEM((sections, cells, ch), F32),
            pltpu.VMEM((steps, cells, ch), F32),
            pltpu.VMEM((rows + 2, cols, 6 * ch), BF16),
            dma((steps,)), dma((6,)), dma((steps,)),
            dma((steps, 2)), dma((steps, 2)), dma((steps, 3)),
            dma((slots, 3)), dma((slots, 2)), dma((slots, 5)), dma((steps, 3)),
            dma((steps, 2)), dma((steps, 2)), dma((steps, 2)), dma((steps, 2)),
        ],
        compiler_params=pltpu.CompilerParams(
            collective_id=0, has_side_effects=True, vmem_limit_bytes=56 * 1024 * 1024
        ),
        name="nowcast",
    )(
        frames.reshape(steps, rows, 2, fine_cols, ch_in),
        patch_weight,
        patch_bias.reshape(1, ch),
        enc_weight,
        cell_weight[0],
        cell_bias,
        head_weight,
    )
    logits = jnp.dot(rounded.reshape(steps * cells, ch), out_weight, preferred_element_type=F32)
    logits = (logits + out_bias).astype(BF16)
    return logits.reshape(1, steps, rows, cols, out_weight.shape[1])


def solution(mesh):
    placed = (
        P("section", None, "space", None, None),
        P(), P(), P(),
        P("section", None, None),
        P("section", None),
        P(), P(), P(),
    )
    return jax.shard_map(
        functools.partial(local, mesh.shape["section"], mesh.shape["space"]),
        mesh=mesh,
        in_specs=placed,
        out_specs=P("section", None, "space", None, None),
        check_vma=False,
    )
```

```python
import functools

import jax
import jax.numpy as jnp
from jax import lax
from jax.experimental import pallas as pl
from jax.experimental.pallas import tpu as pltpu
from jax.sharding import PartitionSpec as P

MESH = pl.DeviceIdType.MESH
BF16 = jnp.bfloat16
F32 = jnp.float32


def sigmoid(x):
    return 0.5 * jnp.tanh(0.5 * x) + 0.5


def shifted(field, by):
    cols = field.shape[1]
    wide = field.astype(F32)
    col = lax.broadcasted_iota(jnp.int32, field.shape, 1)
    left = jnp.where(col >= by, pltpu.roll(wide, by, 1), 0.0).astype(BF16)
    right = jnp.where(col < cols - by, pltpu.roll(wide, cols - by, 1), 0.0).astype(BF16)
    return left, field, right


def kernel(
    sections, spaces,
    frames, pw_hbm, pb_hbm, ew_hbm, cw_hbm, cb_hbm, hw_hbm,
    out_hbm,
    fr, pw, pb, ew, cw, cb, hw, out, proj, ebox, enc, xbox, hbox, gbox, l1box, l2box, mem, resid, joined,
    fr_sem, w_sem, out_sem, e_recv, e_send, enc_send, x_recv, h_recv, u_send, g_recv,
    l1_recv, l1_send, l2_recv, l2_send,
):
    layer = lax.axis_index("section")
    place = lax.axis_index("space")
    last = sections - 1
    has_up = place > 0
    has_down = place < spaces - 1
    above = jnp.maximum(place - 1, 0)
    below = jnp.minimum(place + 1, spaces - 1)
    onward = jnp.minimum(layer + 1, last)
    steps, rows = fr.shape[0], fr.shape[1]
    cols, ch = proj.shape[1] // rows, proj.shape[2]
    cells = rows * cols

    def frame_copy(t):
        return pltpu.make_async_copy(frames.at[t], fr.at[t], fr_sem.at[t])

    pairs = ((pw_hbm, pw), (pb_hbm, pb), (ew_hbm, ew), (cw_hbm, cw), (cb_hbm, cb), (hw_hbm, hw))
    load_pw, load_pb, load_ew, load_cw, load_cb, load_hw = [
        pltpu.make_async_copy(src, dst, w_sem.at[k]) for k, (src, dst) in enumerate(pairs)
    ]
    load_pw.start()
    load_pb.start()
    for t in range(steps):
        frame_copy(t).start()
    for load in (load_ew, load_cw, load_cb, load_hw):
        load.start()

    barrier = pltpu.get_barrier_semaphore()
    for sec in range(sections):
        @pl.when(has_up)
        def _():
            pl.semaphore_signal(barrier, inc=1, device_id=(sec, above), device_id_type=MESH)

        @pl.when(has_down)
        def _():
            pl.semaphore_signal(barrier, inc=1, device_id=(sec, below), device_id_type=MESH)

        @pl.when(layer != sec)
        def _():
            pl.semaphore_signal(barrier, inc=1, device_id=(sec, place), device_id_type=MESH)

    @pl.when(jnp.logical_not(has_up))
    def _():
        for box, depth in ((ebox, 1), (xbox, 1), (hbox, 1), (gbox, 1), (l1box, 2), (l2box, 4)):
            box[:, 0:depth] = jnp.zeros((box.shape[0], depth, cols, ch), BF16)

    @pl.when(jnp.logical_not(has_down))
    def _():
        for box, depth in ((ebox, 1), (xbox, 1), (hbox, 1), (gbox, 1), (l1box, 2), (l2box, 4)):
            end = box.shape[1]
            box[:, end - depth:end] = jnp.zeros((box.shape[0], depth, cols, ch), BF16)

    def send(src, dst, s_sem, r_sem, sec, at):
        return pltpu.make_async_remote_copy(
            src_ref=src, dst_ref=dst, send_sem=s_sem, recv_sem=r_sem,
            device_id=(sec, at), device_id_type=MESH,
        )

    def edges(src, first, dst, depth, s_sem, s_at, r_sem, r_at, sec, go):
        end = dst.shape[0]
        up = send(src.at[pl.ds(first, depth)], dst.at[pl.ds(end - depth, depth)],
                  s_sem(s_at), r_sem(r_at + 1), sec, above)
        down = send(src.at[pl.ds(first + rows - depth, depth)], dst.at[pl.ds(0, depth)],
                    s_sem(s_at + 1), r_sem(r_at), sec, below)

        @pl.when(has_up)
        def _():
            go(up)

        @pl.when(has_down)
        def _():
            go(down)

    def start(copy):
        copy.start()

    def wait_sent(copy):
        copy.wait_send()

    def arrived(ref, sem):
        pltpu.make_async_copy(ref, ref, sem).wait()

    def edges_arrived(box, depth, sem, at):
        end = box.shape[0]

        @pl.when(has_up)
        def _():
            arrived(box.at[pl.ds(0, depth)], sem(at))

        @pl.when(has_down)
        def _():
            arrived(box.at[pl.ds(end - depth, depth)], sem(at + 1))

    def patch(a, b):
        return pw[a, b * ch:(b + 1) * ch, :]

    def ebox_edges(t, go):
        edges(ebox.at[t], 1, ebox.at[t], 1, lambda k: e_send.at[t, k], 0,
              lambda k: e_recv.at[t, k], 0, layer, go)

    def project(t):
        frame_copy(t).wait()
        fine = fr.shape[3]
        place_row = lax.broadcasted_iota(jnp.int32, (fine, fine), 0)
        place_col = lax.broadcasted_iota(jnp.int32, (fine, fine), 1)
        wanted = jnp.where(place_row < cols, 2 * place_row, 2 * place_row - (fine - 1))
        pick = jnp.where(place_col == wanted, 1.0, 0.0).astype(BF16)
        split = []
        for r in range(rows):
            pair = jnp.concatenate([fr[t, r, 0], fr[t, r, 1]], -1)
            both = jnp.dot(pick, pair, preferred_element_type=F32).astype(BF16)
            split.append(jnp.concatenate([both[:cols], both[cols:]], -1))
        weight = jnp.concatenate([patch(a, b) for b in range(2) for a in range(2)], 0)
        total = jnp.dot(jnp.concatenate(split, 0), weight, preferred_element_type=F32) + pb[...]
        rounded = total.astype(BF16)
        proj[t] = rounded
        ebox[t, pl.ds(1, rows)] = jnp.maximum(rounded, jnp.zeros((), BF16)).reshape(rows, cols, ch)

    load_pw.wait()
    load_pb.wait()
    project(0)
    present = 1 + jnp.where(has_up, 1, 0) + jnp.where(has_down, 1, 0)
    pl.semaphore_wait(barrier, sections * present - 1)
    ebox_edges(0, start)

    @pl.loop(1, steps)
    def _(t):
        project(t)
        ebox_edges(t, start)

    def conv(field, weight, by):
        parts = shifted(field, by)
        lhs = jnp.concatenate(
            [part[i * by:i * by + rows].reshape(cells, ch) for i in range(3) for part in parts], -1
        )
        return jnp.dot(lhs, weight, preferred_element_type=F32)

    load_ew.wait()

    def enc_out(t, go):
        slot = t * sections + layer
        edges(enc.at[t], 0, xbox.at[slot], 1, lambda k: enc_send.at[t, k], 0,
              lambda k: x_recv.at[slot, k], 0, 0, go)

    def enc_main(t):
        slot = t * sections + layer
        return send(enc.at[t], xbox.at[slot, pl.ds(1, rows)], enc_send.at[t, 2], x_recv.at[slot, 2], 0, place)

    def encode(t):
        edges_arrived(ebox.at[t], 1, lambda k: e_recv.at[t, k], 0)
        result = proj[t].astype(F32) + conv(ebox[t], ew[...], 1)
        enc[t] = result.astype(BF16).reshape(rows, cols, ch)
        slot = t * sections + layer

        @pl.when(layer == 0)
        def _():
            pltpu.make_async_copy(enc.at[t], xbox.at[slot, pl.ds(1, rows)], x_recv.at[slot, 2]).start()

        @pl.when(layer != 0)
        def _():
            enc_main(t).start()

        enc_out(t, start)

    encode(0)

    @pl.loop(1, steps)
    def _(t):
        @pl.when(layer != 0)
        def _():
            encode(t)

    load_cw.wait()
    load_cb.wait()
    early = min(1, sections - 1)

    def h_edges(slot, go):
        edges(hbox.at[slot], 1, hbox.at[slot], 1, lambda k: u_send.at[slot, k], 0,
              lambda k: h_recv.at[slot, k], 0, layer, go)

    def x_edges(slot, go):
        edges(hbox.at[slot], 1, xbox.at[slot], 1, lambda k: u_send.at[slot, k], 2,
              lambda k: x_recv.at[slot, k], 0, onward, go)

    def g_edges(t, m, go):
        slot = t * sections + m
        edges(hbox.at[slot], 1, gbox.at[t], 1, lambda k: u_send.at[slot, k], 2,
              lambda k: g_recv.at[t, k], 0, m, go)

    def x_main(slot):
        return send(hbox.at[slot, pl.ds(1, rows)], xbox.at[slot, pl.ds(1, rows)],
                    u_send.at[slot, 4], x_recv.at[slot, 2], onward, place)

    def g_main(t, m):
        slot = t * sections + m
        return send(hbox.at[slot, pl.ds(1, rows)], gbox.at[t, pl.ds(1, rows)],
                    u_send.at[slot, 4], g_recv.at[t, 2], m, place)

    def outgoing(t, m, go):
        slot = t * sections + m

        @pl.when(layer < last)
        def _():
            go(x_main(slot))
            x_edges(slot, go)

        @pl.when(layer == last)
        def _():
            @pl.when(m != last)
            def _():
                go(g_main(t, m))

            g_edges(t, m, go)

        @pl.when(t < steps - 1)
        def _():
            h_edges(slot, go)

    def unit(t, m, first):
        slot = t * sections + m
        arrived(xbox.at[slot, pl.ds(1, rows)], x_recv.at[slot, 2])
        edges_arrived(xbox.at[slot], 1, lambda k: x_recv.at[slot, k], 0)
        width = 2 * ch
        if first:
            parts = shifted(xbox[slot], 1)
            for j in range(3):
                joined[:, :, j * ch:(j + 1) * ch] = parts[j]
            lhs = jnp.concatenate(
                [joined[i:i + rows, :, 0:3 * ch].reshape(cells, 3 * ch) for i in range(3)], -1
            )
            weight = jnp.concatenate([cw[k * width:k * width + ch] for k in range(9)], 0)
        else:
            before = slot - sections
            edges_arrived(hbox.at[before], 1, lambda k: h_recv.at[before, k], 0)
            parts = shifted(xbox[slot], 1)
            for j in range(3):
                joined[:, :, j * width:j * width + ch] = parts[j]
            parts = shifted(hbox[before], 1)
            for j in range(3):
                joined[:, :, j * width + ch:(j + 1) * width] = parts[j]
            lhs = jnp.concatenate(
                [joined[i:i + rows].reshape(cells, 3 * width) for i in range(3)], -1
            )
            weight = cw[...]
        z = jnp.dot(lhs, weight, preferred_element_type=F32) + cb[...]
        new = sigmoid(z[:, :ch]) * jnp.tanh(z[:, 2 * ch:3 * ch])
        if not first:
            new = new + sigmoid(z[:, ch:2 * ch]) * mem[m]
        mem[m] = new
        hidden = (sigmoid(z[:, 3 * ch:]) * jnp.tanh(new)).astype(BF16)
        hbox[slot, pl.ds(1, rows)] = hidden.reshape(rows, cols, ch)

        @pl.when(jnp.logical_and(layer == last, m == last))
        def _():
            pltpu.make_async_copy(
                hbox.at[slot, pl.ds(1, rows)], gbox.at[t, pl.ds(1, rows)], g_recv.at[t, 2]
            ).start()

        outgoing(t, m, start)

    @pl.loop(0, sections)
    def _(m):
        unit(0, m, True)

        @pl.when(jnp.logical_and(layer == 0, m == early))
        def _():
            encode(1)

    @pl.loop(1, steps)
    def _(t):
        @pl.loop(0, sections)
        def _(m):
            unit(t, m, False)

            @pl.when(jnp.logical_and(layer == 0, jnp.logical_and(m == early, t < steps - 1)))
            def _():
                encode(t + 1)

    def out_copy(t):
        return pltpu.make_async_copy(out.at[t], out_hbm.at[t], out_sem.at[t])

    load_hw.wait()

    def l1_edges(t, go):
        edges(l1box.at[t], 2, l1box.at[t], 2, lambda k: l1_send.at[t, k], 0,
              lambda k: l1_recv.at[t, k], 0, layer, go)

    def l2_edges(t, go):
        edges(l2box.at[t], 4, l2box.at[t], 4, lambda k: l2_send.at[t, k], 0,
              lambda k: l2_recv.at[t, k], 0, layer, go)

    zero = jnp.zeros((), BF16)

    @pl.loop(0, steps)
    def _(t):
        arrived(gbox.at[t, pl.ds(1, rows)], g_recv.at[t, 2])
        edges_arrived(gbox.at[t], 1, lambda k: g_recv.at[t, k], 0)
        base = gbox[t, pl.ds(1, rows)].reshape(cells, ch).astype(F32)
        y = base + conv(jnp.maximum(gbox[t], zero), hw[0], 1)
        resid[t] = y
        l1box[t, pl.ds(2, rows)] = jnp.maximum(y, 0.0).astype(BF16).reshape(rows, cols, ch)
        l1_edges(t, start)

    @pl.loop(0, steps)
    def _(t):
        edges_arrived(l1box.at[t], 2, lambda k: l1_recv.at[t, k], 0)
        y = resid[t] + conv(l1box[t], hw[1], 2)
        resid[t] = y
        l2box[t, pl.ds(4, rows)] = jnp.maximum(y, 0.0).astype(BF16).reshape(rows, cols, ch)
        l2_edges(t, start)

    @pl.loop(0, steps)
    def _(t):
        edges_arrived(l2box.at[t], 4, lambda k: l2_recv.at[t, k], 0)
        out[t] = (resid[t] + conv(l2box[t], hw[2], 4)).astype(BF16)
        out_copy(t).start()

    for t in range(steps):
        out_copy(t).wait()

    @pl.loop(0, steps)
    def _(t):
        ebox_edges(t, wait_sent)
        enc_out(t, wait_sent)

        @pl.when(layer != 0)
        def _():
            enc_main(t).wait_send()

        l1_edges(t, wait_sent)
        l2_edges(t, wait_sent)

    @pl.loop(0, steps)
    def _(t):
        @pl.loop(0, sections)
        def _(m):
            outgoing(t, m, wait_sent)


def local(sections, spaces, frames, patch_weight, patch_bias, enc_weight, cell_weight,
          cell_bias, head_weight, out_weight, out_bias):
    _, steps, fine_rows, fine_cols, ch_in = frames.shape
    rows, cols = fine_rows // 2, fine_cols // 2
    ch = enc_weight.shape[1]
    cells = rows * cols
    slots = steps * sections
    hbm = pl.BlockSpec(memory_space=pl.ANY)
    dma = pltpu.SemaphoreType.DMA
    rounded = pl.pallas_call(
        functools.partial(kernel, sections, spaces),
        out_shape=jax.ShapeDtypeStruct((steps, cells, ch), BF16),
        in_specs=[hbm] * 7,
        out_specs=hbm,
        scratch_shapes=[
            pltpu.VMEM((steps, rows, 2, fine_cols, ch_in), BF16),
            pltpu.VMEM(patch_weight.shape, BF16),
            pltpu.VMEM((1, ch), F32),
            pltpu.VMEM(enc_weight.shape, BF16),
            pltpu.VMEM(cell_weight.shape[1:], BF16),
            pltpu.VMEM(cell_bias.shape, F32),
            pltpu.VMEM(head_weight.shape, BF16),
            pltpu.VMEM((steps, cells, ch), BF16),
            pltpu.VMEM((steps, cells, ch), BF16),
            pltpu.VMEM((steps, rows + 2, cols, ch), BF16),
            pltpu.VMEM((steps, rows, cols, ch), BF16),
            pltpu.VMEM((slots, rows + 2, cols, ch), BF16),
            pltpu.VMEM((slots, rows + 2, cols, ch), BF16),
            pltpu.VMEM((steps, rows + 2, cols, ch), BF16),
            pltpu.VMEM((steps, rows + 4, cols, ch), BF16),
            pltpu.VMEM((steps, rows + 8, cols, ch), BF16),
            pltpu.VMEM((sections, cells, ch), F32),
            pltpu.VMEM((steps, cells, ch), F32),
            pltpu.VMEM((rows + 2, cols, 6 * ch), BF16),
            dma((steps,)), dma((6,)), dma((steps,)),
            dma((steps, 2)), dma((steps, 2)), dma((steps, 3)),
            dma((slots, 3)), dma((slots, 2)), dma((slots, 5)), dma((steps, 3)),
            dma((steps, 2)), dma((steps, 2)), dma((steps, 2)), dma((steps, 2)),
        ],
        compiler_params=pltpu.CompilerParams(
            collective_id=0, has_side_effects=True, vmem_limit_bytes=56 * 1024 * 1024
        ),
        name="nowcast",
    )(
        frames.reshape(steps, rows, 2, fine_cols, ch_in),
        patch_weight,
        patch_bias.reshape(1, ch),
        enc_weight,
        cell_weight[0],
        cell_bias,
        head_weight,
    )
    logits = jnp.dot(rounded.reshape(steps * cells, ch), out_weight, preferred_element_type=F32)
    logits = (logits + out_bias).astype(BF16)
    return logits.reshape(1, steps, rows, cols, out_weight.shape[1])


def solution(mesh):
    placed = (
        P("section", None, "space", None, None),
        P(), P(), P(),
        P("section", None, None),
        P("section", None),
        P(), P(), P(),
    )
    return jax.shard_map(
        functools.partial(local, mesh.shape["section"], mesh.shape["space"]),
        mesh=mesh,
        in_specs=placed,
        out_specs=P("section", None, "space", None, None),
        check_vma=False,
    )
```

```python
import functools

import jax
import jax.numpy as jnp
from jax import lax
from jax.experimental import pallas as pl
from jax.experimental.pallas import tpu as pltpu
from jax.sharding import PartitionSpec as P

MESH = pl.DeviceIdType.MESH
BF16 = jnp.bfloat16
F32 = jnp.float32


def sigmoid(x):
    return 0.5 * jnp.tanh(0.5 * x) + 0.5


def shifted(field, by):
    cols = field.shape[1]
    wide = field.astype(F32)
    col = lax.broadcasted_iota(jnp.int32, field.shape, 1)
    left = jnp.where(col >= by, pltpu.roll(wide, by, 1), 0.0).astype(BF16)
    right = jnp.where(col < cols - by, pltpu.roll(wide, cols - by, 1), 0.0).astype(BF16)
    return left, field, right


def kernel(
    sections, spaces,
    frames, pw_hbm, pb_hbm, ew_hbm, cw_hbm, cb_hbm, hw_hbm,
    out_hbm,
    fr, pw, pb, ew, cw, cb, hw, out, proj, ebox, enc, xbox, hbox, gbox, l1box, l2box, mem, resid, joined,
    fr_sem, w_sem, out_sem, e_recv, e_send, enc_send, x_recv, h_recv, u_send, g_recv,
    l1_recv, l1_send, l2_recv, l2_send,
):
    layer = lax.axis_index("section")
    place = lax.axis_index("space")
    last = sections - 1
    has_up = place > 0
    has_down = place < spaces - 1
    above = jnp.maximum(place - 1, 0)
    below = jnp.minimum(place + 1, spaces - 1)
    onward = jnp.minimum(layer + 1, last)
    steps, rows = fr.shape[0], fr.shape[1]
    cols, ch = proj.shape[1] // rows, proj.shape[2]
    cells = rows * cols

    def frame_copy(t):
        return pltpu.make_async_copy(frames.at[t], fr.at[t], fr_sem.at[t])

    pairs = ((pw_hbm, pw), (pb_hbm, pb), (ew_hbm, ew), (cw_hbm, cw), (cb_hbm, cb), (hw_hbm, hw))
    load_pw, load_pb, load_ew, load_cw, load_cb, load_hw = [
        pltpu.make_async_copy(src, dst, w_sem.at[k]) for k, (src, dst) in enumerate(pairs)
    ]
    load_pw.start()
    load_pb.start()
    for t in range(steps):
        frame_copy(t).start()
    for load in (load_ew, load_cw, load_cb, load_hw):
        load.start()

    barrier = pltpu.get_barrier_semaphore()
    for sec in range(sections):
        @pl.when(has_up)
        def _():
            pl.semaphore_signal(barrier, inc=1, device_id=(sec, above), device_id_type=MESH)

        @pl.when(has_down)
        def _():
            pl.semaphore_signal(barrier, inc=1, device_id=(sec, below), device_id_type=MESH)

        @pl.when(layer != sec)
        def _():
            pl.semaphore_signal(barrier, inc=1, device_id=(sec, place), device_id_type=MESH)

    @pl.when(jnp.logical_not(has_up))
    def _():
        for box, depth in ((ebox, 1), (xbox, 1), (hbox, 1), (gbox, 1), (l1box, 2), (l2box, 4)):
            box[:, 0:depth] = jnp.zeros((box.shape[0], depth, cols, ch), BF16)

    @pl.when(jnp.logical_not(has_down))
    def _():
        for box, depth in ((ebox, 1), (xbox, 1), (hbox, 1), (gbox, 1), (l1box, 2), (l2box, 4)):
            end = box.shape[1]
            box[:, end - depth:end] = jnp.zeros((box.shape[0], depth, cols, ch), BF16)

    def send(src, dst, s_sem, r_sem, sec, at):
        return pltpu.make_async_remote_copy(
            src_ref=src, dst_ref=dst, send_sem=s_sem, recv_sem=r_sem,
            device_id=(sec, at), device_id_type=MESH,
        )

    def edges(src, first, dst, depth, s_sem, s_at, r_sem, r_at, sec, go):
        end = dst.shape[0]
        up = send(src.at[pl.ds(first, depth)], dst.at[pl.ds(end - depth, depth)],
                  s_sem(s_at), r_sem(r_at + 1), sec, above)
        down = send(src.at[pl.ds(first + rows - depth, depth)], dst.at[pl.ds(0, depth)],
                    s_sem(s_at + 1), r_sem(r_at), sec, below)

        @pl.when(has_up)
        def _():
            go(up)

        @pl.when(has_down)
        def _():
            go(down)

    def start(copy):
        copy.start()

    def wait_sent(copy):
        copy.wait_send()

    def arrived(ref, sem):
        pltpu.make_async_copy(ref, ref, sem).wait()

    def edges_arrived(box, depth, sem, at):
        end = box.shape[0]

        @pl.when(has_up)
        def _():
            arrived(box.at[pl.ds(0, depth)], sem(at))

        @pl.when(has_down)
        def _():
            arrived(box.at[pl.ds(end - depth, depth)], sem(at + 1))

    def patch(a, b):
        return pw[a, b * ch:(b + 1) * ch, :]

    def ebox_edges(t, go):
        edges(ebox.at[t], 1, ebox.at[t], 1, lambda k: e_send.at[t, k], 0,
              lambda k: e_recv.at[t, k], 0, layer, go)

    def project(t):
        frame_copy(t).wait()
        fine = fr.shape[3]
        place_row = lax.broadcasted_iota(jnp.int32, (fine, fine), 0)
        place_col = lax.broadcasted_iota(jnp.int32, (fine, fine), 1)
        wanted = jnp.where(place_row < cols, 2 * place_row, 2 * place_row - (fine - 1))
        pick = jnp.where(place_col == wanted, 1.0, 0.0).astype(BF16)
        split = []
        for r in range(rows):
            pair = jnp.concatenate([fr[t, r, 0], fr[t, r, 1]], -1)
            both = jnp.dot(pick, pair, preferred_element_type=F32).astype(BF16)
            split.append(jnp.concatenate([both[:cols], both[cols:]], -1))
        weight = jnp.concatenate([patch(a, b) for b in range(2) for a in range(2)], 0)
        total = jnp.dot(jnp.concatenate(split, 0), weight, preferred_element_type=F32) + pb[...]
        rounded = total.astype(BF16)
        proj[t] = rounded
        ebox[t, pl.ds(1, rows)] = jnp.maximum(rounded, jnp.zeros((), BF16)).reshape(rows, cols, ch)

    load_pw.wait()
    load_pb.wait()
    project(0)
    present = 1 + jnp.where(has_up, 1, 0) + jnp.where(has_down, 1, 0)
    pl.semaphore_wait(barrier, sections * present - 1)
    ebox_edges(0, start)

    @pl.loop(1, steps)
    def _(t):
        project(t)
        ebox_edges(t, start)

    def conv(field, weight, by):
        parts = shifted(field, by)
        lhs = jnp.concatenate(
            [part[i * by:i * by + rows].reshape(cells, ch) for i in range(3) for part in parts], -1
        )
        return jnp.dot(lhs, weight, preferred_element_type=F32)

    load_ew.wait()

    def enc_out(t, go):
        slot = t * sections + layer
        edges(enc.at[t], 0, xbox.at[slot], 1, lambda k: enc_send.at[t, k], 0,
              lambda k: x_recv.at[slot, k], 0, 0, go)

    def enc_main(t):
        slot = t * sections + layer
        return send(enc.at[t], xbox.at[slot, pl.ds(1, rows)], enc_send.at[t, 2], x_recv.at[slot, 2], 0, place)

    @pl.loop(0, steps)
    def _(t):
        edges_arrived(ebox.at[t], 1, lambda k: e_recv.at[t, k], 0)
        result = proj[t].astype(F32) + conv(ebox[t], ew[...], 1)
        enc[t] = result.astype(BF16).reshape(rows, cols, ch)
        slot = t * sections + layer
        enc_out(t, start)

        @pl.when(layer == 0)
        def _():
            pltpu.make_async_copy(enc.at[t], xbox.at[slot, pl.ds(1, rows)], x_recv.at[slot, 2]).start()

        @pl.when(layer != 0)
        def _():
            enc_main(t).start()

    load_cw.wait()
    load_cb.wait()

    def h_edges(slot, go):
        edges(hbox.at[slot], 1, hbox.at[slot], 1, lambda k: u_send.at[slot, k], 0,
              lambda k: h_recv.at[slot, k], 0, layer, go)

    def x_edges(slot, go):
        edges(hbox.at[slot], 1, xbox.at[slot], 1, lambda k: u_send.at[slot, k], 2,
              lambda k: x_recv.at[slot, k], 0, onward, go)

    def g_edges(t, m, go):
        slot = t * sections + m
        edges(hbox.at[slot], 1, gbox.at[t], 1, lambda k: u_send.at[slot, k], 2,
              lambda k: g_recv.at[t, k], 0, m, go)

    def x_main(slot):
        return send(hbox.at[slot, pl.ds(1, rows)], xbox.at[slot, pl.ds(1, rows)],
                    u_send.at[slot, 4], x_recv.at[slot, 2], onward, place)

    def g_main(t, m):
        slot = t * sections + m
        return send(hbox.at[slot, pl.ds(1, rows)], gbox.at[t, pl.ds(1, rows)],
                    u_send.at[slot, 4], g_recv.at[t, 2], m, place)

    def outgoing(t, m, go):
        slot = t * sections + m

        @pl.when(t < steps - 1)
        def _():
            h_edges(slot, go)

        @pl.when(layer < last)
        def _():
            x_edges(slot, go)
            go(x_main(slot))

        @pl.when(layer == last)
        def _():
            @pl.when(m != last)
            def _():
                go(g_main(t, m))

            g_edges(t, m, go)

    def unit(t, m, first):
        slot = t * sections + m
        arrived(xbox.at[slot, pl.ds(1, rows)], x_recv.at[slot, 2])
        edges_arrived(xbox.at[slot], 1, lambda k: x_recv.at[slot, k], 0)
        width = 2 * ch
        if first:
            parts = shifted(xbox[slot], 1)
            for j in range(3):
                joined[:, :, j * ch:(j + 1) * ch] = parts[j]
            lhs = jnp.concatenate(
                [joined[i:i + rows, :, 0:3 * ch].reshape(cells, 3 * ch) for i in range(3)], -1
            )
            weight = jnp.concatenate([cw[k * width:k * width + ch] for k in range(9)], 0)
        else:
            before = slot - sections
            edges_arrived(hbox.at[before], 1, lambda k: h_recv.at[before, k], 0)
            parts = shifted(xbox[slot], 1)
            for j in range(3):
                joined[:, :, j * width:j * width + ch] = parts[j]
            parts = shifted(hbox[before], 1)
            for j in range(3):
                joined[:, :, j * width + ch:(j + 1) * width] = parts[j]
            lhs = jnp.concatenate(
                [joined[i:i + rows].reshape(cells, 3 * width) for i in range(3)], -1
            )
            weight = cw[...]
        z = jnp.dot(lhs, weight, preferred_element_type=F32) + cb[...]
        new = sigmoid(z[:, :ch]) * jnp.tanh(z[:, 2 * ch:3 * ch])
        if not first:
            new = new + sigmoid(z[:, ch:2 * ch]) * mem[m]
        mem[m] = new
        hidden = (sigmoid(z[:, 3 * ch:]) * jnp.tanh(new)).astype(BF16)
        hbox[slot, pl.ds(1, rows)] = hidden.reshape(rows, cols, ch)

        @pl.when(jnp.logical_and(layer == last, m == last))
        def _():
            pltpu.make_async_copy(
                hbox.at[slot, pl.ds(1, rows)], gbox.at[t, pl.ds(1, rows)], g_recv.at[t, 2]
            ).start()

        outgoing(t, m, start)

    @pl.loop(0, sections)
    def _(m):
        unit(0, m, True)

    @pl.loop(1, steps)
    def _(t):
        @pl.loop(0, sections)
        def _(m):
            unit(t, m, False)

    def out_copy(t):
        return pltpu.make_async_copy(out.at[t], out_hbm.at[t], out_sem.at[t])

    load_hw.wait()

    def l1_edges(t, go):
        edges(l1box.at[t], 2, l1box.at[t], 2, lambda k: l1_send.at[t, k], 0,
              lambda k: l1_recv.at[t, k], 0, layer, go)

    def l2_edges(t, go):
        edges(l2box.at[t], 4, l2box.at[t], 4, lambda k: l2_send.at[t, k], 0,
              lambda k: l2_recv.at[t, k], 0, layer, go)

    zero = jnp.zeros((), BF16)

    @pl.loop(0, steps)
    def _(t):
        arrived(gbox.at[t, pl.ds(1, rows)], g_recv.at[t, 2])
        edges_arrived(gbox.at[t], 1, lambda k: g_recv.at[t, k], 0)
        base = gbox[t, pl.ds(1, rows)].reshape(cells, ch).astype(F32)
        y = base + conv(jnp.maximum(gbox[t], zero), hw[0], 1)
        resid[t] = y
        l1box[t, pl.ds(2, rows)] = jnp.maximum(y, 0.0).astype(BF16).reshape(rows, cols, ch)
        l1_edges(t, start)

    @pl.loop(0, steps)
    def _(t):
        edges_arrived(l1box.at[t], 2, lambda k: l1_recv.at[t, k], 0)
        y = resid[t] + conv(l1box[t], hw[1], 2)
        resid[t] = y
        l2box[t, pl.ds(4, rows)] = jnp.maximum(y, 0.0).astype(BF16).reshape(rows, cols, ch)
        l2_edges(t, start)

    @pl.loop(0, steps)
    def _(t):
        edges_arrived(l2box.at[t], 4, lambda k: l2_recv.at[t, k], 0)
        out[t] = (resid[t] + conv(l2box[t], hw[2], 4)).astype(BF16)
        out_copy(t).start()

    for t in range(steps):
        out_copy(t).wait()

    @pl.loop(0, steps)
    def _(t):
        ebox_edges(t, wait_sent)
        enc_out(t, wait_sent)

        @pl.when(layer != 0)
        def _():
            enc_main(t).wait_send()

        l1_edges(t, wait_sent)
        l2_edges(t, wait_sent)

    @pl.loop(0, steps)
    def _(t):
        @pl.loop(0, sections)
        def _(m):
            outgoing(t, m, wait_sent)


def local(sections, spaces, frames, patch_weight, patch_bias, enc_weight, cell_weight,
          cell_bias, head_weight, out_weight, out_bias):
    _, steps, fine_rows, fine_cols, ch_in = frames.shape
    rows, cols = fine_rows // 2, fine_cols // 2
    ch = enc_weight.shape[1]
    cells = rows * cols
    slots = steps * sections
    hbm = pl.BlockSpec(memory_space=pl.ANY)
    dma = pltpu.SemaphoreType.DMA
    rounded = pl.pallas_call(
        functools.partial(kernel, sections, spaces),
        out_shape=jax.ShapeDtypeStruct((steps, cells, ch), BF16),
        in_specs=[hbm] * 7,
        out_specs=hbm,
        scratch_shapes=[
            pltpu.VMEM((steps, rows, 2, fine_cols, ch_in), BF16),
            pltpu.VMEM(patch_weight.shape, BF16),
            pltpu.VMEM((1, ch), F32),
            pltpu.VMEM(enc_weight.shape, BF16),
            pltpu.VMEM(cell_weight.shape[1:], BF16),
            pltpu.VMEM(cell_bias.shape, F32),
            pltpu.VMEM(head_weight.shape, BF16),
            pltpu.VMEM((steps, cells, ch), BF16),
            pltpu.VMEM((steps, cells, ch), BF16),
            pltpu.VMEM((steps, rows + 2, cols, ch), BF16),
            pltpu.VMEM((steps, rows, cols, ch), BF16),
            pltpu.VMEM((slots, rows + 2, cols, ch), BF16),
            pltpu.VMEM((slots, rows + 2, cols, ch), BF16),
            pltpu.VMEM((steps, rows + 2, cols, ch), BF16),
            pltpu.VMEM((steps, rows + 4, cols, ch), BF16),
            pltpu.VMEM((steps, rows + 8, cols, ch), BF16),
            pltpu.VMEM((sections, cells, ch), F32),
            pltpu.VMEM((steps, cells, ch), F32),
            pltpu.VMEM((rows + 2, cols, 6 * ch), BF16),
            dma((steps,)), dma((6,)), dma((steps,)),
            dma((steps, 2)), dma((steps, 2)), dma((steps, 3)),
            dma((slots, 3)), dma((slots, 2)), dma((slots, 5)), dma((steps, 3)),
            dma((steps, 2)), dma((steps, 2)), dma((steps, 2)), dma((steps, 2)),
        ],
        compiler_params=pltpu.CompilerParams(
            collective_id=0, has_side_effects=True, vmem_limit_bytes=56 * 1024 * 1024
        ),
        name="nowcast",
    )(
        frames.reshape(steps, rows, 2, fine_cols, ch_in),
        patch_weight,
        patch_bias.reshape(1, ch),
        enc_weight,
        cell_weight[0],
        cell_bias,
        head_weight,
    )
    logits = jnp.dot(rounded.reshape(steps * cells, ch), out_weight, preferred_element_type=F32)
    logits = (logits + out_bias).astype(BF16)
    return logits.reshape(1, steps, rows, cols, out_weight.shape[1])


def solution(mesh):
    placed = (
        P("section", None, "space", None, None),
        P(), P(), P(),
        P("section", None, None),
        P("section", None),
        P(), P(), P(),
    )
    return jax.shard_map(
        functools.partial(local, mesh.shape["section"], mesh.shape["space"]),
        mesh=mesh,
        in_specs=placed,
        out_specs=P("section", None, "space", None, None),
        check_vma=False,
    )
```
